32 devices in a mesh: fab: 4 (over y, x), pts: 8 (over z, core).
Axes of the slice: x: 2, y: 2, z: 4, core: 2. Of those that a mesh axis runs over, the one named last changes fastest.
Arguments:
- fabric_params: float32 [8, 512], P(None, 'fab'), may hold values from -1 to 1
- query_points: float32 [3, 16384], P(None, 'pts'), may hold values from -1 to 1
- cotangent: float32 [3, 512, 16384], P(None, 'fab', 'pts'), may hold values from -0.0078125 to 0.0078125
- branch_first: float32 [8, 256], replicated, may hold values from -2 to 2
- branch_second: float32 [256, 256], replicated, may hold values from -0.375 to 0.375
- branch_out: float32 [256, 768], replicated, may hold values from -0.375 to 0.375
- trunk_first: float32 [3, 256], replicated, may hold values from -3.5 to 3.5
- trunk_second: float32 [256, 256], replicated, may hold values from -0.375 to 0.375
- trunk_out: float32 [256, 256], replicated, may hold values from -0.375 to 0.375
Outputs:
- grad_branch_first: float32 [8, 256], replicated
- grad_branch_second: float32 [256, 256], replicated
- grad_branch_out: float32 [256, 768], replicated
- grad_trunk_first: float32 [3, 256], replicated
- grad_trunk_second: float32 [256, 256], replicated
- grad_trunk_out: float32 [256, 256], replicated
The draws below stay inside these ranges and needn't reach their ends.
All inputs are finite; a program needn't handle non-finite values.
Results may differ from the reference program's by a relative error of at most 0.000084.
Values sent between devices are 32-bit elements; how exact they have to be, the bound alone decides.
A program may use at most 64 MiB of HBM per device.

```python
import jax
import jax.numpy as jnp
from jax import lax

KB = 8
H = 256
P_SIZE = 256
FABRICS = 512
POINTS = 16384


def level_of(rng, extent, cuts, smallest, top_value):
    loudness, own = 1.0, jax.random.fold_in(rng, 6)
    for dim, blocks in cuts:
        heights = jnp.exp(jax.random.uniform(jax.random.fold_in(own, dim), (blocks,), jnp.float32, smallest / len(cuts), top_value / len(cuts)))
        loudness = loudness * jnp.repeat(heights, extent[dim] // blocks).reshape([-1 if axis == dim else 1 for axis in range(len(extent))])
    return loudness


def bell_draw(stream_key, shape, deviation, reach, cuts=(), dtype=jnp.bfloat16):
    entries = jax.random.normal(stream_key, shape, jnp.float32) * deviation
    if len(cuts) > 0:
        entries = level_of(stream_key, shape, cuts, -0.22, 0.18) * entries
    return jnp.clip(entries, min=-reach, max=reach).astype(dtype)


def setup_inputs(seed: int = 0) -> dict:
    keys = jax.random.split(jax.random.key(seed), 10)
    return {
        "fabric_params": jnp.clip(jax.random.uniform(keys[0], (KB, FABRICS), jnp.float32, -1.0, 1.0) * level_of(keys[0], (KB, FABRICS), ((1, 4),), -0.4, 0.0), -1.0, 1.0),
        "query_points": jnp.clip(jax.random.uniform(keys[1], (3, POINTS), jnp.float32, -1.0, 1.0) * level_of(keys[1], (3, POINTS), ((1, 8),), -0.4, 0.0), -1.0, 1.0),
        "cotangent": bell_draw(keys[2], (3, FABRICS, POINTS), (FABRICS * POINTS // 16) ** -0.5, 0.0078125, ((1, 4), (2, 8)), jnp.float32),
        "branch_first": bell_draw(keys[3], (KB, H), KB ** -0.5, 2.0, (), jnp.float32),
        "branch_second": bell_draw(keys[4], (H, H), H ** -0.5, 0.375, (), jnp.float32),
        "branch_out": bell_draw(keys[5], (H, 3 * P_SIZE), H ** -0.5, 0.375, (), jnp.float32),
        "trunk_first": jnp.clip(jax.random.uniform(keys[6], (3, H), jnp.float32, -3.5, 3.5), -3.5, 3.5),
        "trunk_second": bell_draw(keys[7], (H, H), H ** -0.5, 0.375, (), jnp.float32),
        "trunk_out": bell_draw(keys[8], (H, P_SIZE), H ** -0.5, 0.375, (), jnp.float32),
    }


HIGH = lax.Precision.HIGHEST


def layers_forward(inputs_t, first, second, out, last_tanh):
    one = jnp.tanh(jnp.einsum("kr,kh->rh", inputs_t, first, precision=HIGH))
    two = jnp.tanh(jnp.dot(one, second, precision=HIGH, preferred_element_type=jnp.float32))
    top = jnp.dot(two, out, precision=HIGH, preferred_element_type=jnp.float32)
    if last_tanh:
        top = jnp.tanh(top)
    return one, two, top


def layers_backward(inputs_t, one, two, top_grad, second, out):
    grad_out = jnp.dot(two.T, top_grad, precision=HIGH, preferred_element_type=jnp.float32)
    dtwo = jnp.dot(top_grad, out.T, precision=HIGH, preferred_element_type=jnp.float32) * (1.0 - two * two)
    grad_second = jnp.dot(one.T, dtwo, precision=HIGH, preferred_element_type=jnp.float32)
    done = jnp.dot(dtwo, second.T, precision=HIGH, preferred_element_type=jnp.float32) * (1.0 - one * one)
    grad_first = jnp.einsum("kr,rh->kh", inputs_t, done, precision=HIGH)
    return grad_first, grad_second, grad_out


def reference(fabric_params, query_points, cotangent, branch_first, branch_second, branch_out, trunk_first, trunk_second, trunk_out):
    hb1, hb2, coef = layers_forward(fabric_params, branch_first, branch_second, branch_out, False)
    ht1, ht2, basis = layers_forward(query_points, trunk_first, trunk_second, trunk_out, True)
    fab_count = coef.shape[0]
    width = basis.shape[1]
    coef_grad = jnp.einsum("cfn,np->fcp", cotangent, basis, precision=HIGH).reshape(fab_count, 3 * width)
    basis_grad = jnp.einsum("cfn,fcp->np", cotangent, coef.reshape(fab_count, 3, width), precision=HIGH)
    gb1, gb2, gb3 = layers_backward(fabric_params, hb1, hb2, coef_grad, branch_second, branch_out)
    top_grad = basis_grad * (1.0 - basis * basis)
    gt1, gt2, gt3 = layers_backward(query_points, ht1, ht2, top_grad, trunk_second, trunk_out)
    return gb1, gb2, gb3, gt1, gt2, gt3
```

```python
import jax
import jax.numpy as jnp
from jax import lax
from jax.sharding import PartitionSpec as P

HIGH = lax.Precision.HIGH


def layers_forward(inputs_t, first, second, out, last_tanh):
    one = jnp.tanh(jnp.einsum("kr,kh->rh", inputs_t, first, precision=HIGH))
    two = jnp.tanh(jnp.dot(one, second, precision=HIGH, preferred_element_type=jnp.float32))
    top = jnp.dot(two, out, precision=HIGH, preferred_element_type=jnp.float32)
    if last_tanh:
        top = jnp.tanh(top)
    return (one, two, top)


def layers_backward(inputs_t, one, two, top_grad, second, out):
    grad_out = jnp.dot(two.T, top_grad, precision=HIGH, preferred_element_type=jnp.float32)
    dtwo = jnp.dot(top_grad, out.T, precision=HIGH, preferred_element_type=jnp.float32) * (
        1.0 - two * two
    )
    grad_second = jnp.dot(one.T, dtwo, precision=HIGH, preferred_element_type=jnp.float32)
    done = jnp.dot(dtwo, second.T, precision=HIGH, preferred_element_type=jnp.float32) * (
        1.0 - one * one
    )
    grad_first = jnp.einsum("kr,rh->kh", inputs_t, done, precision=HIGH)
    return (grad_first, grad_second, grad_out)


def local(
    fabric_params,
    query_points,
    cotangent,
    branch_first,
    branch_second,
    branch_out,
    trunk_first,
    trunk_second,
    trunk_out,
):
    hb1, hb2, coef = layers_forward(fabric_params, branch_first, branch_second, branch_out, False)
    ht1, ht2, basis = layers_forward(query_points, trunk_first, trunk_second, trunk_out, True)
    fab_local = coef.shape[0]
    width = basis.shape[1]
    coef_split = coef.reshape(fab_local, 3, width)
    basis_grad = jnp.einsum("cfn,fcp->np", cotangent, coef_split, precision=HIGH)
    top_grad = basis_grad * (1.0 - basis * basis)
    local_trunk = layers_backward(query_points, ht1, ht2, top_grad, trunk_second, trunk_out)
    coef_grad = jnp.einsum("cfn,np->fcp", cotangent, basis, precision=HIGH).reshape(fab_local, 3 * width)
    local_branch = layers_backward(fabric_params, hb1, hb2, coef_grad, branch_second, branch_out)
    gb1, gb2, gb3, gt1, gt2, gt3 = lax.psum(local_branch + local_trunk, ("fab", "pts"))
    return (gb1, gb2, gb3, gt1, gt2, gt3)


def solution(mesh):
    return jax.shard_map(
        local,
        mesh=mesh,
        in_specs=(
            P(None, "fab"),
            P(None, "pts"),
            P(None, "fab", "pts"),
            P(),
            P(),
            P(),
            P(),
            P(),
            P(),
        ),
        out_specs=(P(), P(), P(), P(), P(), P()),
        check_vma=False,
    )
```

```python
import functools

import jax
import jax.numpy as jnp
from jax import lax
from jax.experimental import pallas as pl
from jax.experimental.pallas import tpu as pltpu
from jax.sharding import PartitionSpec as P

HIGH = lax.Precision.HIGH
MESH = pl.DeviceIdType.MESH
LANES = 128


def layers_forward(inputs_t, first, second, out, last_tanh):
    one = jnp.tanh(jnp.einsum("kr,kh->rh", inputs_t, first, precision=HIGH))
    two = jnp.tanh(jnp.dot(one, second, precision=HIGH, preferred_element_type=jnp.float32))
    top = jnp.dot(two, out, precision=HIGH, preferred_element_type=jnp.float32)
    if last_tanh:
        top = jnp.tanh(top)
    return (one, two, top)


def layers_backward(inputs_t, one, two, top_grad, second, out):
    grad_out = jnp.dot(two.T, top_grad, precision=HIGH, preferred_element_type=jnp.float32)
    dtwo = jnp.dot(top_grad, out.T, precision=HIGH, preferred_element_type=jnp.float32) * (
        1.0 - two * two
    )
    grad_second = jnp.dot(one.T, dtwo, precision=HIGH, preferred_element_type=jnp.float32)
    done = jnp.dot(dtwo, second.T, precision=HIGH, preferred_element_type=jnp.float32) * (
        1.0 - one * one
    )
    grad_first = jnp.einsum("kr,rh->kh", inputs_t, done, precision=HIGH)
    return (grad_first, grad_second, grad_out)


class Plan:
    def __init__(self, rows, nf, nq):
        self.nf, self.nq = nf, nq
        unit = 8 * nf * nq
        units = -(-rows // (2 * unit))
        a = max(1, (9 * units + 6) // 13)
        self.ra, self.rb = a * unit, (units - a) * unit
        self.half = self.ra + self.rb
        self.total = 2 * self.half
        self.pa, self.pb = self.ra // nf, self.rb // nq
        self.sa, self.sb = self.pa // nq, self.pb // nf
        self.count = 1 + 2 * 2 * (nf - 1 + nq - 1) + nf + nq

    def scratch(self):
        f32 = jnp.float32
        return [
            pltpu.VMEM((self.total, LANES), f32),
            pltpu.VMEM((self.total, LANES), f32),
            pltpu.VMEM((self.half, LANES), f32),
            pltpu.VMEM((max(self.nf - 1, 1), self.pa, LANES), f32),
            pltpu.VMEM((max(self.nq - 1, 1), max(self.pb, 8), LANES), f32),
            pltpu.VMEM((max(self.nq - 1, 1), self.sa, LANES), f32),
            pltpu.VMEM((max(self.nf - 1, 1), max(self.sb, 8), LANES), f32),
            pltpu.SemaphoreType.DMA((self.count,)),
            pltpu.SemaphoreType.DMA((self.count,)),
        ]


def where(plan):
    f = lax.axis_index("fab")
    p = lax.axis_index("pts")
    return f, p // 2, p % 2


def greet(plan):
    f, q, c = where(plan)
    barrier = pltpu.get_barrier_semaphore()
    peers = [(f, 2 * q + 1 - c)]
    peers += [(lax.rem(f + k, plan.nf), 2 * q + c) for k in range(1, plan.nf)]
    peers += [(f, 2 * lax.rem(q + k, plan.nq) + c) for k in range(1, plan.nq)]
    for peer in peers:
        pl.semaphore_signal(barrier, inc=1, device_id=peer, device_id_type=MESH)
    pl.semaphore_wait(barrier, len(peers))


def sum_over_all(plan, acc, res, core_in, a1, b1, a2, b2, send, recv):
    nf, nq = plan.nf, plan.nq
    ra, pa, sa, pb, sb = plan.ra, plan.pa, plan.sa, plan.pb, plan.sb
    f, q, c = where(plan)
    has_b = plan.rb > 0
    used, started = [0], []

    def rows(start, size):
        return pl.ds(pl.multiple_of(start, 8), size)

    def go(src, dst, peer):
        index = used[0]
        used[0] += 1
        copy = pltpu.make_async_remote_copy(
            src_ref=src,
            dst_ref=dst,
            send_sem=send.at[index],
            recv_sem=recv.at[index],
            device_id=peer,
            device_id_type=MESH,
        )
        copy.start()
        started.append(copy)
        return copy

    def fab_peers():
        return [(k, lax.rem(f + k, nf)) for k in range(1, nf)]

    def pts_peers():
        return [(k, lax.rem(q + k, nq)) for k in range(1, nq)]

    def at_fab(d):
        return (d, 2 * q + c)

    def at_pts(d):
        return (f, 2 * d + c)

    sibling = (f, 2 * q + 1 - c)
    mine = c * plan.half
    other = (1 - c) * plan.half

    go(acc.at[rows(other, plan.half)], core_in, sibling).wait_recv()
    acc[rows(mine, plan.half), :] += core_in[...]

    base_a = mine + f * pa
    base_b = mine + ra + q * pb
    own_a = base_a + q * sa
    own_b = base_b + f * sb

    first_a = [go(acc.at[rows(mine + d * pa, pa)], a1.at[k - 1], at_fab(d)) for k, d in fab_peers()]
    first_b = []
    if has_b:
        first_b = [
            go(acc.at[rows(mine + ra + d * pb, pb)], b1.at[k - 1], at_pts(d)) for k, d in pts_peers()
        ]

    def add_up(into, start, size, slots, copies):
        value = acc[rows(start, size), :]
        for k, copy in enumerate(copies):
            copy.wait_recv()
            value = value + slots[k]
        into[rows(start, size), :] = value

    add_up(acc, base_a, pa, a1, first_a)
    second_a = [go(acc.at[rows(base_a + d * sa, sa)], a2.at[k - 1], at_pts(d)) for k, d in pts_peers()]
    second_b = []
    if has_b:
        add_up(acc, base_b, pb, b1, first_b)
        second_b = [
            go(acc.at[rows(base_b + d * sb, sb)], b2.at[k - 1], at_fab(d)) for k, d in fab_peers()
        ]

    def give(start, size, peer):
        part = res.at[rows(start, size)]
        return go(part, part, peer)

    add_up(res, own_a, sa, a2, second_a)
    third_a = [give(own_a, sa, at_pts(d)) for _, d in pts_peers()]
    third_b = []
    if has_b:
        add_up(res, own_b, sb, b2, second_b)
        third_b = [give(own_b, sb, at_fab(d)) for _, d in fab_peers()]

    last = []
    for copy in third_a:
        copy.wait_recv()
    fourth_a = [give(base_a, pa, at_fab(d)) for _, d in fab_peers()]
    last.append(give(base_a, pa, sibling))
    fourth_b = []
    if has_b:
        for copy in third_b:
            copy.wait_recv()
        fourth_b = [give(base_b, pb, at_pts(d)) for _, d in pts_peers()]
        last.append(give(base_b, pb, sibling))
    for k, copy in enumerate(fourth_a):
        copy.wait_recv()
        last.append(give(mine + lax.rem(f + nf - 1 - k, nf) * pa, pa, sibling))
    for k, copy in enumerate(fourth_b):
        copy.wait_recv()
        last.append(give(mine + ra + lax.rem(q + nq - 1 - k, nq) * pb, pb, sibling))
    for copy in last:
        copy.wait_recv()
    for copy in started:
        copy.wait_send()


def pieces(shapes):
    table, start = [], 0
    for i, (r, w) in enumerate(shapes):
        kept = -(-r // 8) * 8
        for col in range(0, w, LANES):
            table.append((i, col, r, kept, start))
            start += kept
    return table, start


def sum_kernel(plan, table, n, *refs):
    ins, outs = refs[:n], refs[n : 2 * n]
    acc, res, *rest = refs[2 * n :]
    greet(plan)
    acc[...] = jnp.zeros_like(acc)
    for i, col, r, _, start in table:
        acc[start : start + r, :] = ins[i][:, col : col + LANES]
    sum_over_all(plan, acc, res, *rest)
    for i, col, r, _, start in table:
        outs[i][:, col : col + LANES] = res[start : start + r, :]


def summed(grads, nf, nq):
    shapes = [g.shape for g in grads]
    table, rows = pieces(shapes)
    plan = Plan(rows, nf, nq)
    vmem = pl.BlockSpec(memory_space=pltpu.VMEM)
    return pl.pallas_call(
        functools.partial(sum_kernel, plan, table, len(grads)),
        out_shape=[jax.ShapeDtypeStruct(s, jnp.float32) for s in shapes],
        in_specs=[vmem] * len(grads),
        out_specs=[vmem] * len(grads),
        scratch_shapes=plan.scratch(),
        compiler_params=pltpu.CompilerParams(
            collective_id=0, has_side_effects=True, vmem_limit_bytes=40 * 1024 * 1024
        ),
    )(*grads)


def local(
    nf,
    nq,
    fabric_params,
    query_points,
    cotangent,
    branch_first,
    branch_second,
    branch_out,
    trunk_first,
    trunk_second,
    trunk_out,
):
    hb1, hb2, coef = layers_forward(fabric_params, branch_first, branch_second, branch_out, False)
    ht1, ht2, basis = layers_forward(query_points, trunk_first, trunk_second, trunk_out, True)
    fab_local = coef.shape[0]
    width = basis.shape[1]
    coef_split = coef.reshape(fab_local, 3, width)
    basis_grad = jnp.einsum("cfn,fcp->np", cotangent, coef_split, precision=HIGH)
    top_grad = basis_grad * (1.0 - basis * basis)
    local_trunk = layers_backward(query_points, ht1, ht2, top_grad, trunk_second, trunk_out)
    coef_grad = jnp.einsum("cfn,np->fcp", cotangent, basis, precision=HIGH).reshape(
        fab_local, 3 * width
    )
    local_branch = layers_backward(fabric_params, hb1, hb2, coef_grad, branch_second, branch_out)
    return tuple(summed(local_branch + local_trunk, nf, nq))


def solution(mesh):
    nf = mesh.shape["fab"]
    nq = mesh.shape["pts"] // 2
    return jax.shard_map(
        functools.partial(local, nf, nq),
        mesh=mesh,
        in_specs=(
            P(None, "fab"),
            P(None, "pts"),
            P(None, "fab", "pts"),
            P(),
            P(),
            P(),
            P(),
            P(),
            P(),
        ),
        out_specs=(P(), P(), P(), P(), P(), P()),
        check_vma=False,
    )
```

```python
import functools

import jax
import jax.numpy as jnp
from jax import lax
from jax.experimental import pallas as pl
from jax.experimental.pallas import tpu as pltpu
from jax.sharding import PartitionSpec as P

MESH = pl.DeviceIdType.MESH
LANES = 128


def split(value):
    high = value.astype(jnp.bfloat16)
    return high, (value - high.astype(jnp.float32)).astype(jnp.bfloat16)


def dot(left, right, left_dim=1, right_dim=0):
    lefts = jnp.concatenate([left[0], left[0], left[1]], axis=left_dim)
    rights = jnp.concatenate([right[0], right[1], right[0]], axis=right_dim)
    return lax.dot_general(
        lefts, rights, (((left_dim,), (right_dim,)), ((), ())), preferred_element_type=jnp.float32
    )


class Plan:
    def __init__(self, rows, nf, nq):
        self.nf, self.nq = nf, nq
        unit = 8 * nf * nq
        units = -(-rows // (2 * unit))
        a = max(1, (9 * units + 6) // 13) if units > 1 else 1
        self.ra, self.rb = a * unit, (units - a) * unit
        self.half = self.ra + self.rb
        self.total = 2 * self.half
        self.pa, self.pb = self.ra // nf, self.rb // nq
        self.sa, self.sb = self.pa // nq, self.pb // nf
        self.count = 1 + 2 * 2 * (nf - 1 + nq - 1) + nf + nq

    def scratch(self):
        f32 = jnp.float32
        return [
            pltpu.VMEM((self.total, LANES), f32),
            pltpu.VMEM((self.total, LANES), f32),
            pltpu.VMEM((self.half, LANES), f32),
            pltpu.VMEM((max(self.nf - 1, 1), self.pa, LANES), f32),
            pltpu.VMEM((max(self.nq - 1, 1), max(self.pb, 8), LANES), f32),
            pltpu.VMEM((max(self.nq - 1, 1), self.sa, LANES), f32),
            pltpu.VMEM((max(self.nf - 1, 1), max(self.sb, 8), LANES), f32),
            pltpu.SemaphoreType.DMA((self.count,)),
            pltpu.SemaphoreType.DMA((self.count,)),
        ]


def where(plan):
    f = lax.axis_index("fab")
    p = lax.axis_index("pts")
    return f, p // 2, p % 2


def greet(plan):
    f, q, c = where(plan)
    barrier = pltpu.get_barrier_semaphore()
    peers = [(f, 2 * q + 1 - c)]
    peers += [(lax.rem(f + k, plan.nf), 2 * q + c) for k in range(1, plan.nf)]
    peers += [(f, 2 * lax.rem(q + k, plan.nq) + c) for k in range(1, plan.nq)]
    for peer in peers:
        pl.semaphore_signal(barrier, inc=1, device_id=peer, device_id_type=MESH)
    pl.semaphore_wait(barrier, len(peers))


def sum_over_all(plan, acc, res, core_in, a1, b1, a2, b2, send, recv):
    nf, nq = plan.nf, plan.nq
    ra, pa, sa, pb, sb = plan.ra, plan.pa, plan.sa, plan.pb, plan.sb
    f, q, c = where(plan)
    has_b = plan.rb > 0
    used, started = [0], []

    def rows(start, size):
        return pl.ds(pl.multiple_of(start, 8), size)

    def go(src, dst, peer):
        index = used[0]
        used[0] += 1
        copy = pltpu.make_async_remote_copy(
            src_ref=src,
            dst_ref=dst,
            send_sem=send.at[index],
            recv_sem=recv.at[index],
            device_id=peer,
            device_id_type=MESH,
        )
        copy.start()
        started.append(copy)
        return copy

    def fab_peers():
        return [(k, lax.rem(f + k, nf)) for k in range(1, nf)]

    def pts_peers():
        return [(k, lax.rem(q + k, nq)) for k in range(1, nq)]

    def at_fab(d):
        return (d, 2 * q + c)

    def at_pts(d):
        return (f, 2 * d + c)

    sibling = (f, 2 * q + 1 - c)
    mine = c * plan.half
    other = (1 - c) * plan.half

    core = go(acc.at[rows(other, plan.half)], core_in, sibling)
    yield
    core.wait_recv()
    acc[rows(mine, plan.half), :] += core_in[...]

    base_a = mine + f * pa
    base_b = mine + ra + q * pb
    own_a = base_a + q * sa
    own_b = base_b + f * sb

    first_a = [go(acc.at[rows(mine + d * pa, pa)], a1.at[k - 1], at_fab(d)) for k, d in fab_peers()]
    first_b = []
    if has_b:
        first_b = [
            go(acc.at[rows(mine + ra + d * pb, pb)], b1.at[k - 1], at_pts(d)) for k, d in pts_peers()
        ]

    yield

    def add_up(into, start, size, slots, copies):
        value = acc[rows(start, size), :]
        for k, copy in enumerate(copies):
            copy.wait_recv()
            value = value + slots[k]
        into[rows(start, size), :] = value

    add_up(acc, base_a, pa, a1, first_a)
    second_a = [go(acc.at[rows(base_a + d * sa, sa)], a2.at[k - 1], at_pts(d)) for k, d in pts_peers()]
    second_b = []
    if has_b:
        add_up(acc, base_b, pb, b1, first_b)
        second_b = [
            go(acc.at[rows(base_b + d * sb, sb)], b2.at[k - 1], at_fab(d)) for k, d in fab_peers()
        ]

    yield

    def give(start, size, peer):
        part = res.at[rows(start, size)]
        return go(part, part, peer)

    add_up(res, own_a, sa, a2, second_a)
    third_a = [give(own_a, sa, at_pts(d)) for _, d in pts_peers()]
    third_b = []
    if has_b:
        add_up(res, own_b, sb, b2, second_b)
        third_b = [give(own_b, sb, at_fab(d)) for _, d in fab_peers()]

    yield

    last = []
    for copy in third_a:
        copy.wait_recv()
    fourth_a = [give(base_a, pa, at_fab(d)) for _, d in fab_peers()]
    last.append(give(base_a, pa, sibling))
    fourth_b = []
    if has_b:
        for copy in third_b:
            copy.wait_recv()
        fourth_b = [give(base_b, pb, at_pts(d)) for _, d in pts_peers()]
        last.append(give(base_b, pb, sibling))
    yield
    for k, copy in enumerate(fourth_a):
        copy.wait_recv()
        last.append(give(mine + lax.rem(f + nf - 1 - k, nf) * pa, pa, sibling))
    for k, copy in enumerate(fourth_b):
        copy.wait_recv()
        last.append(give(mine + ra + lax.rem(q + nq - 1 - k, nq) * pb, pb, sibling))
    yield
    for copy in last:
        copy.wait_recv()
    for copy in started:
        copy.wait_send()


def pieces(shapes):
    table, start = [], 0
    for i, (r, w) in enumerate(shapes):
        kept = -(-r // 8) * 8
        for col in range(0, w, LANES):
            table.append((i, col, r, kept, start))
            start += kept
    return table, start


def kernel(
    plan_b,
    plan_t,
    table_b,
    table_t,
    fp_ref,
    q_ref,
    cot_ref,
    b1_ref,
    b2_ref,
    b3_ref,
    t1_ref,
    t2_ref,
    t3_ref,
    out_b,
    out_t,
    cot,
    cot_sem,
    cot_hi,
    cot_lo,
    coef_hi,
    coef_lo,
    h1_hi,
    h1_lo,
    h2_hi,
    h2_lo,
    d1,
    d2,
    d3,
    t2_split,
    t3_split,
    t2_turned,
    t3_turned,
    first_turned,
    q_pad,
    coef_grad,
    g_first,
    g_second,
    g_out,
    *comm,
):
    half = len(comm) // 2
    acc_b, res_b, *rest_b = comm[:half]
    acc_t, res_t, *rest_t = comm[half:]
    load = pltpu.make_async_copy(cot_ref, cot, cot_sem)
    load.start()

    fab_local = fp_ref.shape[1]
    points = q_ref.shape[1]
    hidden, width = t3_ref.shape
    step = min(points, 512)
    steps = points // step
    kq, kb = q_ref.shape[0], fp_ref.shape[0]

    def keep(pair_ref, value):
        pair_ref[0], pair_ref[1] = split(value)

    def pair(ref):
        return ref[0], ref[1]

    q_pad[...] = jnp.zeros_like(q_pad)
    q_pad[0:kq, :] = q_ref[...]
    g_first[...] = jnp.zeros_like(g_first)
    g_first[0:kq, :] = t1_ref[...]
    first_turned[...] = g_first[...].T
    keep(t2_split, t2_ref[...])
    keep(t3_split, t3_ref[...])
    keep(t2_turned, t2_ref[...].T)
    keep(t3_turned, t3_ref[...].T)

    fp_turned = fp_ref[...].T
    pre = fp_turned[:, 0:1] * b1_ref[0:1, :]
    for k in range(1, kb):
        pre += fp_turned[:, k : k + 1] * b1_ref[k : k + 1, :]
    hb1 = jnp.tanh(pre)
    b2 = split(b2_ref[...])
    hb2 = jnp.tanh(dot(split(hb1), b2))
    b3 = split(b3_ref[...])
    coef = dot(split(hb2), b3)
    comps = coef.shape[1] // width
    turned = jnp.concatenate([coef[:, c * width : (c + 1) * width].T for c in range(comps)], axis=1)
    coef_hi[...], coef_lo[...] = split(turned)

    coef_grad[...] = jnp.zeros_like(coef_grad)
    load.wait()

    def forward(i, carry):
        xs = pl.ds(pl.multiple_of(i * step, step), step)
        pre = first_turned[:, 0:1] * q_pad[0:1, xs]
        for k in range(1, kq):
            pre += first_turned[:, k : k + 1] * q_pad[k : k + 1, xs]
        one = jnp.tanh(pre)
        d1[:, xs] = 1.0 - one * one
        one = split(one)
        h1_hi[:, xs], h1_lo[:, xs] = one
        two = jnp.tanh(dot(pair(t2_turned), one))
        d2[:, xs] = 1.0 - two * two
        two = split(two)
        h2_hi[:, xs], h2_lo[:, xs] = two
        basis = jnp.tanh(dot(pair(t3_turned), two))
        d3[:, xs] = 1.0 - basis * basis
        cots = split(cot[:, xs])
        cot_hi[:, xs], cot_lo[:, xs] = cots
        coef_grad[...] += dot(cots, split(basis), 1, 1)
        return carry

    lax.fori_loop(0, steps, forward, 0)

    top = jnp.concatenate(
        [coef_grad[c * fab_local : (c + 1) * fab_local, :] for c in range(comps)], axis=1
    )
    top = split(top)
    gb3 = dot(split(hb2.T), top)
    db2 = split(dot(top, b3, 1, 1) * (1.0 - hb2 * hb2))
    gb2 = dot(split(hb1.T), db2)
    for values, i in ((gb2, 0), (gb3, 1)):
        for j, col, r, _, start in table_b:
            if j == i:
                acc_b[start : start + r, :] = values[:, col : col + LANES]
    tail = table_b[-1][4] + table_b[-1][3]
    if tail < plan_b.total:
        acc_b[tail:, :] = jnp.zeros((plan_b.total - tail, LANES), jnp.float32)
    greet(plan_b)
    sum_b = sum_over_all(plan_b, acc_b, res_b, *rest_b)
    next(sum_b)
    db1 = dot(db2, b2, 1, 1) * (1.0 - hb1 * hb1)
    gb1 = dot(split(fp_ref[...]), split(db1))

    g_first[...] = jnp.zeros_like(g_first)
    g_second[...] = jnp.zeros_like(g_second)
    g_out[...] = jnp.zeros_like(g_out)

    def backward(i):
        xs = pl.ds(i * step, step)
        three = dot((coef_hi[...], coef_lo[...]), (cot_hi[:, xs], cot_lo[:, xs])) * d3[:, xs]
        three = split(three)
        g_out[...] += dot((h2_hi[:, xs], h2_lo[:, xs]), three, 1, 1)
        two = split(dot(pair(t3_split), three) * d2[:, xs])
        g_second[...] += dot((h1_hi[:, xs], h1_lo[:, xs]), two, 1, 1)
        one = split(dot(pair(t2_split), two) * d1[:, xs])
        g_first[...] += dot(split(q_pad[:, xs]), one, 1, 1)

    cuts = [0, steps // 4, steps // 2, steps]
    for low, high in zip(cuts, cuts[1:]):
        for i in range(low, high):
            backward(i)
        if high < steps:
            next(sum_b)

    parts = (gb1, g_first[...], g_second[...], g_out[...])
    for i, col, r, kept, start in table_t:
        acc_t[start : start + kept, :] = parts[i][0:kept, col : col + LANES]
    tail = table_t[-1][4] + table_t[-1][3]
    if tail < plan_t.total:
        acc_t[tail:, :] = jnp.zeros((plan_t.total - tail, LANES), jnp.float32)
    sums = [sum_over_all(plan_t, acc_t, res_t, *rest_t), sum_b]
    while sums:
        for one in list(sums):
            if next(one, True):
                sums.remove(one)
    out_b[...] = res_b[...]
    out_t[...] = res_t[...]


def unpack(tables, shapes, flat_b, flat_t, *outs):
    for flat, table, group in zip((flat_b, flat_t), tables, shapes):
        for i, col, r, _, start in table:
            outs[group[i]][:, col : col + LANES] = flat[start : start + r, :]


def local(nf, nq, fabric_params, query_points, cotangent, b1, b2, b3, t1, t2, t3):
    comps, fab_local, points = cotangent.shape
    cot = cotangent.reshape(comps * fab_local, points)
    shapes = [w.shape for w in (b1, b2, b3, t1, t2, t3)]
    group_b, group_t = (1, 2), (0, 3, 4, 5)
    table_b, rows_b = pieces([shapes[i] for i in group_b])
    table_t, rows_t = pieces([shapes[i] for i in group_t])
    plan_b, plan_t = Plan(rows_b, nf, nq), Plan(rows_t, nf, nq)
    hidden, width = t3.shape
    vmem = pl.BlockSpec(memory_space=pltpu.VMEM)
    f32, bf16 = jnp.float32, jnp.bfloat16
    rows = comps * fab_local
    flat_b, flat_t = pl.pallas_call(
        functools.partial(kernel, plan_b, plan_t, table_b, table_t),
        out_shape=[
            jax.ShapeDtypeStruct((plan_b.total, LANES), f32),
            jax.ShapeDtypeStruct((plan_t.total, LANES), f32),
        ],
        in_specs=[vmem, vmem, pl.BlockSpec(memory_space=pl.ANY)] + [vmem] * 6,
        out_specs=[vmem] * 2,
        scratch_shapes=[
            pltpu.VMEM((rows, points), f32),
            pltpu.SemaphoreType.DMA,
            pltpu.VMEM((rows, points), bf16),
            pltpu.VMEM((rows, points), bf16),
            pltpu.VMEM((width, rows), bf16),
            pltpu.VMEM((width, rows), bf16),
            pltpu.VMEM((hidden, points), bf16),
            pltpu.VMEM((hidden, points), bf16),
            pltpu.VMEM((hidden, points), bf16),
            pltpu.VMEM((hidden, points), bf16),
            pltpu.VMEM((hidden, points), f32),
            pltpu.VMEM((hidden, points), f32),
            pltpu.VMEM((width, points), f32),
            pltpu.VMEM((2,) + t2.shape, bf16),
            pltpu.VMEM((2,) + t3.shape, bf16),
            pltpu.VMEM((2,) + t2.shape[::-1], bf16),
            pltpu.VMEM((2,) + t3.shape[::-1], bf16),
            pltpu.VMEM((hidden, 8), f32),
            pltpu.VMEM((8, points), f32),
            pltpu.VMEM((rows, width), f32),
            pltpu.VMEM((8, hidden), f32),
            pltpu.VMEM(t2.shape, f32),
            pltpu.VMEM(t3.shape, f32),
        ]
        + plan_b.scratch()
        + plan_t.scratch(),
        compiler_params=pltpu.CompilerParams(
            collective_id=0, has_side_effects=True, vmem_limit_bytes=50 * 1024 * 1024
        ),
    )(fabric_params, query_points, cot, b1, b2, b3, t1, t2, t3)
    return tuple(
        pl.pallas_call(
            functools.partial(unpack, (table_b, table_t), (group_b, group_t)),
            out_shape=[jax.ShapeDtypeStruct(s, f32) for s in shapes],
            in_specs=[vmem] * 2,
            out_specs=[vmem] * 6,
        )(flat_b, flat_t)
    )


def solution(mesh):
    nf = mesh.shape["fab"]
    nq = mesh.shape["pts"] // 2
    return jax.shard_map(
        functools.partial(local, nf, nq),
        mesh=mesh,
        in_specs=(
            P(None, "fab"),
            P(None, "pts"),
            P(None, "fab", "pts"),
            P(),
            P(),
            P(),
            P(),
            P(),
            P(),
        ),
        out_specs=(P(), P(), P(), P(), P(), P()),
        check_vma=False,
    )
```

```python
import functools

import jax
import jax.numpy as jnp
from jax import lax
from jax.experimental import pallas as pl
from jax.experimental.pallas import tpu as pltpu
from jax.sharding import PartitionSpec as P

MESH = pl.DeviceIdType.MESH
LANES = 128


def split(value):
    high = value.astype(jnp.bfloat16)
    return high, (value - high.astype(jnp.float32)).astype(jnp.bfloat16)


def dot(left, right, left_dim=1, right_dim=0):
    lefts = jnp.concatenate([left[0], left[0], left[1]], axis=left_dim)
    rights = jnp.concatenate([right[0], right[1], right[0]], axis=right_dim)
    return lax.dot_general(
        lefts, rights, (((left_dim,), (right_dim,)), ((), ())), preferred_element_type=jnp.float32
    )


class Plan:
    def __init__(self, rows, nf, nq):
        self.nf, self.nq = nf, nq
        unit = 8 * nf * nq
        units = -(-rows // (2 * unit))
        a = max(1, (9 * units + 6) // 13) if units > 1 else 1
        self.ra, self.rb = a * unit, (units - a) * unit
        self.half = self.ra + self.rb
        self.total = 2 * self.half
        self.pa, self.pb = self.ra // nf, self.rb // nq
        self.sa, self.sb = self.pa // nq, self.pb // nf
        self.count = 1 + 2 * 2 * (nf - 1 + nq - 1) + nf + nq

    def scratch(self):
        f32 = jnp.float32
        return [
            pltpu.VMEM((self.total, LANES), f32),
            pltpu.VMEM((self.total, LANES), f32),
            pltpu.VMEM((self.half, LANES), f32),
            pltpu.VMEM((max(self.nf - 1, 1), self.pa, LANES), f32),
            pltpu.VMEM((max(self.nq - 1, 1), max(self.pb, 8), LANES), f32),
            pltpu.VMEM((max(self.nq - 1, 1), self.sa, LANES), f32),
            pltpu.VMEM((max(self.nf - 1, 1), max(self.sb, 8), LANES), f32),
            pltpu.SemaphoreType.DMA((self.count,)),
            pltpu.SemaphoreType.DMA((self.count,)),
        ]


def where(plan):
    f = lax.axis_index("fab")
    p = lax.axis_index("pts")
    return f, p // 2, p % 2


def greet(plan):
    f, q, c = where(plan)
    barrier = pltpu.get_barrier_semaphore()
    peers = [(f, 2 * q + 1 - c)]
    peers += [(lax.rem(f + k, plan.nf), 2 * q + c) for k in range(1, plan.nf)]
    peers += [(f, 2 * lax.rem(q + k, plan.nq) + c) for k in range(1, plan.nq)]
    for peer in peers:
        pl.semaphore_signal(barrier, inc=1, device_id=peer, device_id_type=MESH)


def met(plan):
    pl.semaphore_wait(pltpu.get_barrier_semaphore(), plan.nf + plan.nq - 1)


def sum_over_all(plan, acc, res, core_in, a1, b1, a2, b2, send, recv):
    nf, nq = plan.nf, plan.nq
    ra, pa, sa, pb, sb = plan.ra, plan.pa, plan.sa, plan.pb, plan.sb
    f, q, c = where(plan)
    has_b = plan.rb > 0
    used, started = [0], []

    def rows(start, size):
        return pl.ds(pl.multiple_of(start, 8), size)

    def go(src, dst, peer):
        index = used[0]
        used[0] += 1
        copy = pltpu.make_async_remote_copy(
            src_ref=src,
            dst_ref=dst,
            send_sem=send.at[index],
            recv_sem=recv.at[index],
            device_id=peer,
            device_id_type=MESH,
        )
        copy.start()
        started.append(copy)
        return copy

    def fab_peers():
        return [(k, lax.rem(f + k, nf)) for k in range(1, nf)]

    def pts_peers():
        return [(k, lax.rem(q + k, nq)) for k in range(1, nq)]

    def at_fab(d):
        return (d, 2 * q + c)

    def at_pts(d):
        return (f, 2 * d + c)

    sibling = (f, 2 * q + 1 - c)
    mine = c * plan.half
    other = (1 - c) * plan.half

    core = go(acc.at[rows(other, plan.half)], core_in, sibling)
    yield
    core.wait_recv()
    acc[rows(mine, plan.half), :] += core_in[...]

    base_a = mine + f * pa
    base_b = mine + ra + q * pb
    own_a = base_a + q * sa
    own_b = base_b + f * sb

    first_a = [go(acc.at[rows(mine + d * pa, pa)], a1.at[k - 1], at_fab(d)) for k, d in fab_peers()]
    first_b = []
    if has_b:
        first_b = [
            go(acc.at[rows(mine + ra + d * pb, pb)], b1.at[k - 1], at_pts(d)) for k, d in pts_peers()
        ]

    yield

    def add_up(into, start, size, slots, copies):
        value = acc[rows(start, size), :]
        for k, copy in enumerate(copies):
            copy.wait_recv()
            value = value + slots[k]
        into[rows(start, size), :] = value

    add_up(acc, base_a, pa, a1, first_a)
    second_a = [go(acc.at[rows(base_a + d * sa, sa)], a2.at[k - 1], at_pts(d)) for k, d in pts_peers()]
    second_b = []
    if has_b:
        add_up(acc, base_b, pb, b1, first_b)
        second_b = [
            go(acc.at[rows(base_b + d * sb, sb)], b2.at[k - 1], at_fab(d)) for k, d in fab_peers()
        ]

    yield

    def give(start, size, peer):
        part = res.at[rows(start, size)]
        return go(part, part, peer)

    add_up(res, own_a, sa, a2, second_a)
    third_a = [give(own_a, sa, at_pts(d)) for _, d in pts_peers()]
    third_b = []
    if has_b:
        add_up(res, own_b, sb, b2, second_b)
        third_b = [give(own_b, sb, at_fab(d)) for _, d in fab_peers()]

    yield

    last = []
    for copy in third_a:
        copy.wait_recv()
    fourth_a = [give(base_a, pa, at_fab(d)) for _, d in fab_peers()]
    last.append(give(base_a, pa, sibling))
    fourth_b = []
    if has_b:
        for copy in third_b:
            copy.wait_recv()
        fourth_b = [give(base_b, pb, at_pts(d)) for _, d in pts_peers()]
        last.append(give(base_b, pb, sibling))
    yield
    for k, copy in enumerate(fourth_a):
        copy.wait_recv()
        last.append(give(mine + lax.rem(f + nf - 1 - k, nf) * pa, pa, sibling))
    for k, copy in enumerate(fourth_b):
        copy.wait_recv()
        last.append(give(mine + ra + lax.rem(q + nq - 1 - k, nq) * pb, pb, sibling))
    yield
    for copy in last:
        copy.wait_recv()
    for copy in started:
        copy.wait_send()


def pieces(shapes):
    table, start = [], 0
    for i, (r, w) in enumerate(shapes):
        kept = -(-r // 8) * 8
        for col in range(0, w, LANES):
            table.append((i, col, r, kept, start))
            start += kept
    return table, start


def kernel(
    plan_b,
    plan_t,
    table_b,
    table_t,
    *refs,
):
    given, outs, held = refs[:9], refs[9:11], refs[11:20]
    loads = [
        pltpu.make_async_copy(src, dst, refs[20].at[i])
        for i, (src, dst) in enumerate(zip(given, held))
    ]
    for i in (6, 1, 7, 8, 0, 3, 4, 5, 2):
        loads[i].start()
    greet(plan_b)
    compute(plan_b, plan_t, table_b, table_t, loads, *outs, refs[21], *held, *refs[22:])


def compute(
    plan_b,
    plan_t,
    table_b,
    table_t,
    loads,
    out_b,
    out_t,
    out_sem,
    fp_ref,
    q_ref,
    cot,
    b1_ref,
    b2_ref,
    b3_ref,
    t1_ref,
    t2_ref,
    t3_ref,
    cot_hi,
    cot_lo,
    coef_hi,
    coef_lo,
    h1_hi,
    h1_lo,
    h2_hi,
    h2_lo,
    d1,
    d2,
    d3,
    t2_split,
    t3_split,
    t2_turned,
    t3_turned,
    first_turned,
    q_pad,
    coef_grad,
    g_first,
    g_second,
    g_out,
    *comm,
):
    half = len(comm) // 2
    acc_b, res_b, *rest_b = comm[:half]
    acc_t, res_t, *rest_t = comm[half:]

    for i in (6, 1, 7, 8):
        loads[i].wait()
    fab_local = fp_ref.shape[1]
    points = q_ref.shape[1]
    hidden, width = t3_ref.shape
    step = min(points, 512)
    steps = points // step
    kq, kb = q_ref.shape[0], fp_ref.shape[0]

    def keep(pair_ref, value):
        pair_ref[0], pair_ref[1] = split(value)

    def pair(ref):
        return ref[0], ref[1]

    q_pad[...] = jnp.zeros_like(q_pad)
    q_pad[0:kq, :] = q_ref[...]
    g_first[...] = jnp.zeros_like(g_first)
    g_first[0:kq, :] = t1_ref[...]
    first_turned[...] = g_first[...].T
    keep(t2_split, t2_ref[...])
    keep(t3_split, t3_ref[...])
    keep(t2_turned, t2_ref[...].T)
    keep(t3_turned, t3_ref[...].T)

    for i in (0, 3, 4, 5):
        loads[i].wait()

    fp_turned = fp_ref[...].T
    pre = fp_turned[:, 0:1] * b1_ref[0:1, :]
    for k in range(1, kb):
        pre += fp_turned[:, k : k + 1] * b1_ref[k : k + 1, :]
    hb1 = jnp.tanh(pre)
    b2 = split(b2_ref[...])
    hb2 = jnp.tanh(dot(split(hb1), b2))
    b3 = split(b3_ref[...])
    coef = dot(split(hb2), b3)
    comps = coef.shape[1] // width
    turned = jnp.concatenate([coef[:, c * width : (c + 1) * width].T for c in range(comps)], axis=1)
    coef_hi[...], coef_lo[...] = split(turned)

    coef_grad[...] = jnp.zeros_like(coef_grad)
    loads[2].wait()

    def forward(i, carry):
        xs = pl.ds(pl.multiple_of(i * step, step), step)
        pre = first_turned[:, 0:1] * q_pad[0:1, xs]
        for k in range(1, kq):
            pre += first_turned[:, k : k + 1] * q_pad[k : k + 1, xs]
        one = jnp.tanh(pre)
        d1[:, xs] = 1.0 - one * one
        one = split(one)
        h1_hi[:, xs], h1_lo[:, xs] = one
        two = jnp.tanh(dot(pair(t2_turned), one))
        d2[:, xs] = 1.0 - two * two
        two = split(two)
        h2_hi[:, xs], h2_lo[:, xs] = two
        basis = jnp.tanh(dot(pair(t3_turned), two))
        d3[:, xs] = 1.0 - basis * basis
        cots = split(cot[:, xs])
        cot_hi[:, xs], cot_lo[:, xs] = cots
        coef_grad[...] += dot(cots, split(basis), 1, 1)
        return carry

    lax.fori_loop(0, steps, forward, 0)

    top = jnp.concatenate(
        [coef_grad[c * fab_local : (c + 1) * fab_local, :] for c in range(comps)], axis=1
    )
    top = split(top)
    gb3 = dot(split(hb2.T), top)
    db2 = split(dot(top, b3, 1, 1) * (1.0 - hb2 * hb2))
    gb2 = dot(split(hb1.T), db2)
    for values, i in ((gb2, 0), (gb3, 1)):
        for j, col, r, _, start in table_b:
            if j == i:
                acc_b[start : start + r, :] = values[:, col : col + LANES]
    tail = table_b[-1][4] + table_b[-1][3]
    if tail < plan_b.total:
        acc_b[tail:, :] = jnp.zeros((plan_b.total - tail, LANES), jnp.float32)
    met(plan_b)
    sum_b = sum_over_all(plan_b, acc_b, res_b, *rest_b)
    next(sum_b)
    db1 = dot(db2, b2, 1, 1) * (1.0 - hb1 * hb1)
    gb1 = dot(split(fp_ref[...]), split(db1))

    g_first[...] = jnp.zeros_like(g_first)
    g_second[...] = jnp.zeros_like(g_second)
    g_out[...] = jnp.zeros_like(g_out)

    def backward(i):
        xs = pl.ds(i * step, step)
        three = dot((coef_hi[...], coef_lo[...]), (cot_hi[:, xs], cot_lo[:, xs])) * d3[:, xs]
        three = split(three)
        g_out[...] += dot((h2_hi[:, xs], h2_lo[:, xs]), three, 1, 1)
        two = split(dot(pair(t3_split), three) * d2[:, xs])
        g_second[...] += dot((h1_hi[:, xs], h1_lo[:, xs]), two, 1, 1)
        one = split(dot(pair(t2_split), two) * d1[:, xs])
        g_first[...] += dot(split(q_pad[:, xs]), one, 1, 1)

    cuts = [0, steps // 4, steps]
    for low, high in zip(cuts, cuts[1:]):
        for i in range(low, high):
            backward(i)
        if high < steps:
            next(sum_b)

    parts = (gb1, g_first[...], g_second[...], g_out[...])
    for i, col, r, kept, start in table_t:
        acc_t[start : start + kept, :] = parts[i][0:kept, col : col + LANES]
    tail = table_t[-1][4] + table_t[-1][3]
    if tail < plan_t.total:
        acc_t[tail:, :] = jnp.zeros((plan_t.total - tail, LANES), jnp.float32)
    sums = [sum_over_all(plan_t, acc_t, res_t, *rest_t), sum_b]
    stores = (
        pltpu.make_async_copy(res_t, out_t, out_sem.at[0]),
        pltpu.make_async_copy(res_b, out_b, out_sem.at[1]),
    )
    while any(sums):
        for i, one in enumerate(sums):
            if one is not None and next(one, True):
                stores[i].start()
                sums[i] = None
    for store in stores:
        store.wait()


def unpack(tables, groups, flat_b, flat_t, *refs):
    outs, small, sems = refs[:6], refs[6], refs[7]
    first = pltpu.make_async_copy(flat_t.at[pl.ds(0, small.shape[0])], small, sems.at[0])
    first.start()
    copies = []
    for flat, table, group in zip((flat_b, flat_t), tables, groups):
        for i, col, r, _, start in table:
            if group[i] not in (0, 3):
                copies.append(
                    pltpu.make_async_copy(
                        flat.at[pl.ds(start, r)],
                        outs[group[i]].at[:, pl.ds(col, LANES)],
                        sems.at[1 + len(copies)],
                    )
                )
                copies[-1].start()
    first.wait()
    for i, col, r, _, start in tables[1]:
        if groups[1][i] in (0, 3):
            outs[groups[1][i]][:, col : col + LANES] = small[start : start + r, :]
    for copy in copies:
        copy.wait()


def local(nf, nq, fabric_params, query_points, cotangent, b1, b2, b3, t1, t2, t3):
    comps, fab_local, points = cotangent.shape
    cot = cotangent.reshape(comps * fab_local, points)
    shapes = [w.shape for w in (b1, b2, b3, t1, t2, t3)]
    group_b, group_t = (1, 2), (0, 3, 4, 5)
    table_b, rows_b = pieces([shapes[i] for i in group_b])
    table_t, rows_t = pieces([shapes[i] for i in group_t])
    plan_b, plan_t = Plan(rows_b, nf, nq), Plan(rows_t, nf, nq)
    hidden, width = t3.shape
    vmem = pl.BlockSpec(memory_space=pltpu.VMEM)
    hbm = pl.BlockSpec(memory_space=pl.ANY)
    small = sum(kept for i, _, _, kept, _ in table_t if group_t[i] in (0, 3))
    f32, bf16 = jnp.float32, jnp.bfloat16
    rows = comps * fab_local
    flat_b, flat_t = pl.pallas_call(
        functools.partial(kernel, plan_b, plan_t, table_b, table_t),
        out_shape=[
            jax.ShapeDtypeStruct((plan_b.total, LANES), f32),
            jax.ShapeDtypeStruct((plan_t.total, LANES), f32),
        ],
        in_specs=[hbm] * 9,
        out_specs=[hbm] * 2,
        scratch_shapes=[
            *[
                pltpu.VMEM(x.shape, f32)
                for x in (fabric_params, query_points, cot, b1, b2, b3, t1, t2, t3)
            ],
            pltpu.SemaphoreType.DMA((9,)),
            pltpu.SemaphoreType.DMA((2,)),
            pltpu.VMEM((rows, points), bf16),
            pltpu.VMEM((rows, points), bf16),
            pltpu.VMEM((width, rows), bf16),
            pltpu.VMEM((width, rows), bf16),
            pltpu.VMEM((hidden, points), bf16),
            pltpu.VMEM((hidden, points), bf16),
            pltpu.VMEM((hidden, points), bf16),
            pltpu.VMEM((hidden, points), bf16),
            pltpu.VMEM((hidden, points), f32),
            pltpu.VMEM((hidden, points), f32),
            pltpu.VMEM((width, points), f32),
            pltpu.VMEM((2,) + t2.shape, bf16),
            pltpu.VMEM((2,) + t3.shape, bf16),
            pltpu.VMEM((2,) + t2.shape[::-1], bf16),
            pltpu.VMEM((2,) + t3.shape[::-1], bf16),
            pltpu.VMEM((hidden, 8), f32),
            pltpu.VMEM((8, points), f32),
            pltpu.VMEM((rows, width), f32),
            pltpu.VMEM((8, hidden), f32),
            pltpu.VMEM(t2.shape, f32),
            pltpu.VMEM(t3.shape, f32),
        ]
        + plan_b.scratch()
        + plan_t.scratch(),
        compiler_params=pltpu.CompilerParams(
            collective_id=0, has_side_effects=True, vmem_limit_bytes=50 * 1024 * 1024
        ),
    )(fabric_params, query_points, cot, b1, b2, b3, t1, t2, t3)
    return tuple(
        pl.pallas_call(
            functools.partial(unpack, (table_b, table_t), (group_b, group_t)),
            out_shape=[jax.ShapeDtypeStruct(s, f32) for s in shapes],
            in_specs=[hbm] * 2,
            out_specs=[vmem if i in (0, 3) else hbm for i in range(6)],
            scratch_shapes=[
                pltpu.VMEM((small, LANES), f32),
                pltpu.SemaphoreType.DMA((1 + len(table_b) + len(table_t),)),
            ],
        )(flat_b, flat_t)
    )


def solution(mesh):
    nf = mesh.shape["fab"]
    nq = mesh.shape["pts"] // 2
    return jax.shard_map(
        functools.partial(local, nf, nq),
        mesh=mesh,
        in_specs=(
            P(None, "fab"),
            P(None, "pts"),
            P(None, "fab", "pts"),
            P(),
            P(),
            P(),
            P(),
            P(),
            P(),
        ),
        out_specs=(P(), P(), P(), P(), P(), P()),
        check_vma=False,
    )
```

```python
import functools

import jax
import jax.numpy as jnp
from jax import lax
from jax.experimental import pallas as pl
from jax.experimental.pallas import tpu as pltpu
from jax.sharding import PartitionSpec as P

MESH = pl.DeviceIdType.MESH
LANES = 128


def split(value):
    high = value.astype(jnp.bfloat16)
    return high, (value - high.astype(jnp.float32)).astype(jnp.bfloat16)


def dot(left, right, left_dim=1, right_dim=0):
    lefts = jnp.concatenate([left[0], left[0], left[1]], axis=left_dim)
    rights = jnp.concatenate([right[0], right[1], right[0]], axis=right_dim)
    return lax.dot_general(
        lefts, rights, (((left_dim,), (right_dim,)), ((), ())), preferred_element_type=jnp.float32
    )


class Plan:
    def __init__(self, rows, nf, nq):
        self.nf, self.nq = nf, nq
        unit = 8 * nf * nq
        units = -(-rows // (2 * unit))
        a = max(1, (9 * units + 6) // 13) if units > 1 else 1
        self.ra, self.rb = a * unit, (units - a) * unit
        self.half = self.ra + self.rb
        self.total = 2 * self.half
        self.pa, self.pb = self.ra // nf, self.rb // nq
        self.sa, self.sb = self.pa // nq, self.pb // nf
        self.count = 1 + 2 * 2 * (nf - 1 + nq - 1) + nf + nq

    def scratch(self):
        f32 = jnp.float32
        return [
            pltpu.VMEM((self.total, LANES), f32),
            pltpu.VMEM((self.total, LANES), f32),
            pltpu.VMEM((self.half, LANES), f32),
            pltpu.VMEM((max(self.nf - 1, 1), self.pa, LANES), f32),
            pltpu.VMEM((max(self.nq - 1, 1), max(self.pb, 8), LANES), f32),
            pltpu.VMEM((max(self.nq - 1, 1), self.sa, LANES), f32),
            pltpu.VMEM((max(self.nf - 1, 1), max(self.sb, 8), LANES), f32),
            pltpu.SemaphoreType.DMA((self.count,)),
            pltpu.SemaphoreType.DMA((self.count,)),
        ]


def where(plan):
    f = lax.axis_index("fab")
    p = lax.axis_index("pts")
    return f, p // 2, p % 2


def greet(plan):
    f, q, c = where(plan)
    barrier = pltpu.get_barrier_semaphore()
    peers = [(f, 2 * q + 1 - c)]
    peers += [(lax.rem(f + k, plan.nf), 2 * q + c) for k in range(1, plan.nf)]
    peers += [(f, 2 * lax.rem(q + k, plan.nq) + c) for k in range(1, plan.nq)]
    for peer in peers:
        pl.semaphore_signal(barrier, inc=1, device_id=peer, device_id_type=MESH)


def met(plan):
    pl.semaphore_wait(pltpu.get_barrier_semaphore(), plan.nf + plan.nq - 1)


def sum_over_all(plan, acc, res, core_in, a1, b1, a2, b2, send, recv):
    nf, nq = plan.nf, plan.nq
    ra, pa, sa, pb, sb = plan.ra, plan.pa, plan.sa, plan.pb, plan.sb
    f, q, c = where(plan)
    has_b = plan.rb > 0
    used, started = [0], []

    def rows(start, size):
        return pl.ds(pl.multiple_of(start, 8), size)

    def go(src, dst, peer):
        index = used[0]
        used[0] += 1
        copy = pltpu.make_async_remote_copy(
            src_ref=src,
            dst_ref=dst,
            send_sem=send.at[index],
            recv_sem=recv.at[index],
            device_id=peer,
            device_id_type=MESH,
        )
        copy.start()
        started.append(copy)
        return copy

    def fab_peers():
        return [(k, lax.rem(f + k, nf)) for k in range(1, nf)]

    def pts_peers():
        return [(k, lax.rem(q + k, nq)) for k in range(1, nq)]

    def at_fab(d):
        return (d, 2 * q + c)

    def at_pts(d):
        return (f, 2 * d + c)

    sibling = (f, 2 * q + 1 - c)
    mine = c * plan.half
    other = (1 - c) * plan.half

    core = go(acc.at[rows(other, plan.half)], core_in, sibling)
    yield
    core.wait_recv()
    acc[rows(mine, plan.half), :] += core_in[...]

    base_a = mine + f * pa
    base_b = mine + ra + q * pb
    own_a = base_a + q * sa
    own_b = base_b + f * sb

    first_a = [go(acc.at[rows(mine + d * pa, pa)], a1.at[k - 1], at_fab(d)) for k, d in fab_peers()]
    first_b = []
    if has_b:
        first_b = [
            go(acc.at[rows(mine + ra + d * pb, pb)], b1.at[k - 1], at_pts(d)) for k, d in pts_peers()
        ]

    yield

    def add_up(into, start, size, slots, copies):
        value = acc[rows(start, size), :]
        for k, copy in enumerate(copies):
            copy.wait_recv()
            value = value + slots[k]
        into[rows(start, size), :] = value

    add_up(acc, base_a, pa, a1, first_a)
    second_a = [go(acc.at[rows(base_a + d * sa, sa)], a2.at[k - 1], at_pts(d)) for k, d in pts_peers()]
    second_b = []
    if has_b:
        add_up(acc, base_b, pb, b1, first_b)
        second_b = [
            go(acc.at[rows(base_b + d * sb, sb)], b2.at[k - 1], at_fab(d)) for k, d in fab_peers()
        ]

    yield

    def give(start, size, peer):
        part = res.at[rows(start, size)]
        return go(part, part, peer)

    add_up(res, own_a, sa, a2, second_a)
    third_a = [give(own_a, sa, at_pts(d)) for _, d in pts_peers()]
    third_b = []
    if has_b:
        add_up(res, own_b, sb, b2, second_b)
        third_b = [give(own_b, sb, at_fab(d)) for _, d in fab_peers()]

    yield

    last = []
    for copy in third_a:
        copy.wait_recv()
    fourth_a = [give(base_a, pa, at_fab(d)) for _, d in fab_peers()]
    last.append(give(base_a, pa, sibling))
    fourth_b = []
    if has_b:
        for copy in third_b:
            copy.wait_recv()
        fourth_b = [give(base_b, pb, at_pts(d)) for _, d in pts_peers()]
        last.append(give(base_b, pb, sibling))
    yield
    for k, copy in enumerate(fourth_a):
        copy.wait_recv()
        last.append(give(mine + lax.rem(f + nf - 1 - k, nf) * pa, pa, sibling))
    for k, copy in enumerate(fourth_b):
        copy.wait_recv()
        last.append(give(mine + ra + lax.rem(q + nq - 1 - k, nq) * pb, pb, sibling))
    yield
    for copy in last:
        copy.wait_recv()
    for copy in started:
        copy.wait_send()


def pieces(shapes):
    table, start = [], 0
    for i, (r, w) in enumerate(shapes):
        kept = -(-r // 8) * 8
        for col in range(0, w, LANES):
            table.append((i, col, r, kept, start))
            start += kept
    return table, start


def kernel(
    plan_b,
    plan_t,
    table_b,
    table_t,
    *refs,
):
    given, outs, held = refs[:9], refs[9:11], refs[11:20]
    loads = [
        pltpu.make_async_copy(src, dst, refs[20].at[i])
        for i, (src, dst) in enumerate(zip(given, held))
    ]
    for i in (6, 1, 7, 8, 0, 3, 4, 5, 2):
        loads[i].start()
    greet(plan_b)
    compute(plan_b, plan_t, table_b, table_t, loads, *outs, refs[21], *held, *refs[22:])


def compute(
    plan_b,
    plan_t,
    table_b,
    table_t,
    loads,
    out_b,
    out_t,
    out_sem,
    fp_ref,
    q_ref,
    cot,
    b1_ref,
    b2_ref,
    b3_ref,
    t1_ref,
    t2_ref,
    t3_ref,
    cot_hi,
    cot_lo,
    coef_hi,
    coef_lo,
    h1_hi,
    h1_lo,
    h2_hi,
    h2_lo,
    d1,
    d2,
    d3,
    t2_split,
    t3_split,
    t2_turned,
    t3_turned,
    first_turned,
    q_pad,
    coef_grad,
    g_first,
    g_second,
    g_out,
    *comm,
):
    half = len(comm) // 2
    acc_b, res_b, *rest_b = comm[:half]
    acc_t, res_t, *rest_t = comm[half:]

    for i in (6, 1, 7, 8):
        loads[i].wait()
    fab_local = fp_ref.shape[1]
    points = q_ref.shape[1]
    hidden, width = t3_ref.shape
    step = min(points, 512)
    steps = points // step
    kq, kb = q_ref.shape[0], fp_ref.shape[0]

    def keep(pair_ref, value):
        pair_ref[0], pair_ref[1] = split(value)

    def pair(ref):
        return ref[0], ref[1]

    q_pad[...] = jnp.zeros_like(q_pad)
    q_pad[0:kq, :] = q_ref[...]
    g_first[...] = jnp.zeros_like(g_first)
    g_first[0:kq, :] = t1_ref[...]
    first_turned[...] = g_first[...].T
    keep(t2_split, t2_ref[...])
    keep(t3_split, t3_ref[...])
    keep(t2_turned, t2_ref[...].T)
    keep(t3_turned, t3_ref[...].T)

    for i in (0, 3, 4, 5):
        loads[i].wait()

    fp_turned = fp_ref[...].T
    pre = fp_turned[:, 0:1] * b1_ref[0:1, :]
    for k in range(1, kb):
        pre += fp_turned[:, k : k + 1] * b1_ref[k : k + 1, :]
    hb1 = jnp.tanh(pre)
    b2 = split(b2_ref[...])
    hb2 = jnp.tanh(dot(split(hb1), b2))
    b3 = split(b3_ref[...])
    coef = dot(split(hb2), b3)
    comps = coef.shape[1] // width
    turned = jnp.concatenate([coef[:, c * width : (c + 1) * width].T for c in range(comps)], axis=1)
    coef_hi[...], coef_lo[...] = split(turned)

    coef_grad[...] = jnp.zeros_like(coef_grad)
    loads[2].wait()

    def forward(i, carry):
        xs = pl.ds(pl.multiple_of(i * step, step), step)
        pre = first_turned[:, 0:1] * q_pad[0:1, xs]
        for k in range(1, kq):
            pre += first_turned[:, k : k + 1] * q_pad[k : k + 1, xs]
        one = jnp.tanh(pre)
        d1[:, xs] = 1.0 - one * one
        one = split(one)
        h1_hi[:, xs], h1_lo[:, xs] = one
        two = jnp.tanh(dot(pair(t2_turned), one))
        d2[:, xs] = 1.0 - two * two
        two = split(two)
        h2_hi[:, xs], h2_lo[:, xs] = two
        basis = jnp.tanh(dot(pair(t3_turned), two))
        d3[:, xs] = 1.0 - basis * basis
        cots = split(cot[:, xs])
        cot_hi[:, xs], cot_lo[:, xs] = cots
        coef_grad[...] += dot(cots, split(basis), 1, 1)
        return carry

    lax.fori_loop(0, steps, forward, 0)

    top = jnp.concatenate(
        [coef_grad[c * fab_local : (c + 1) * fab_local, :] for c in range(comps)], axis=1
    )
    top = split(top)
    gb3 = dot(split(hb2.T), top)
    db2 = split(dot(top, b3, 1, 1) * (1.0 - hb2 * hb2))
    gb2 = dot(split(hb1.T), db2)
    for values, i in ((gb2, 0), (gb3, 1)):
        for j, col, r, _, start in table_b:
            if j == i:
                acc_b[start : start + r, :] = values[:, col : col + LANES]
    tail = table_b[-1][4] + table_b[-1][3]
    if tail < plan_b.total:
        acc_b[tail:, :] = jnp.zeros((plan_b.total - tail, LANES), jnp.float32)
    met(plan_b)
    sum_b = sum_over_all(plan_b, acc_b, res_b, *rest_b)
    next(sum_b)
    db1 = dot(db2, b2, 1, 1) * (1.0 - hb1 * hb1)
    gb1 = dot(split(fp_ref[...]), split(db1))

    g_first[...] = jnp.zeros_like(g_first)
    g_second[...] = jnp.zeros_like(g_second)
    g_out[...] = jnp.zeros_like(g_out)

    def backward(i):
        xs = pl.ds(i * step, step)
        three = dot((coef_hi[...], coef_lo[...]), (cot_hi[:, xs], cot_lo[:, xs])) * d3[:, xs]
        three = split(three)
        g_out[...] += dot((h2_hi[:, xs], h2_lo[:, xs]), three, 1, 1)
        two = split(dot(pair(t3_split), three) * d2[:, xs])
        g_second[...] += dot((h1_hi[:, xs], h1_lo[:, xs]), two, 1, 1)
        one = split(dot(pair(t2_split), two) * d1[:, xs])
        g_first[...] += dot(split(q_pad[:, xs]), one, 1, 1)

    cuts = [0, steps // 4, steps]
    for low, high in zip(cuts, cuts[1:]):
        for i in range(low, high):
            backward(i)
        if high < steps:
            next(sum_b)

    parts = (gb1, g_first[...], g_second[...], g_out[...])
    for i, col, r, kept, start in table_t:
        acc_t[start : start + kept, :] = parts[i][0:kept, col : col + LANES]
    tail = table_t[-1][4] + table_t[-1][3]
    if tail < plan_t.total:
        acc_t[tail:, :] = jnp.zeros((plan_t.total - tail, LANES), jnp.float32)
    sums = [sum_over_all(plan_t, acc_t, res_t, *rest_t), sum_b]
    stores = (
        pltpu.make_async_copy(res_t, out_t, out_sem.at[0]),
        pltpu.make_async_copy(res_b, out_b, out_sem.at[1]),
    )
    while any(sums):
        for i, one in enumerate(sums):
            if one is not None and next(one, True):
                stores[i].start()
                sums[i] = None
    for store in stores:
        store.wait()


def unpack(tables, groups, flat_b, flat_t, *refs):
    outs, held, sems = refs[:6], refs[6:8], refs[8]
    loads = [pltpu.make_async_copy((flat_b, flat_t)[i], held[i], sems.at[i]) for i in range(2)]
    for load in loads:
        load.start()
    for load, flat, table, group in zip(loads, held, tables, groups):
        load.wait()
        for i, col, r, _, start in table:
            outs[group[i]][:, col : col + LANES] = flat[start : start + r, :]


def local(nf, nq, fabric_params, query_points, cotangent, b1, b2, b3, t1, t2, t3):
    comps, fab_local, points = cotangent.shape
    cot = cotangent.reshape(comps * fab_local, points)
    shapes = [w.shape for w in (b1, b2, b3, t1, t2, t3)]
    group_b, group_t = (1, 2), (0, 3, 4, 5)
    table_b, rows_b = pieces([shapes[i] for i in group_b])
    table_t, rows_t = pieces([shapes[i] for i in group_t])
    plan_b, plan_t = Plan(rows_b, nf, nq), Plan(rows_t, nf, nq)
    hidden, width = t3.shape
    vmem = pl.BlockSpec(memory_space=pltpu.VMEM)
    hbm = pl.BlockSpec(memory_space=pltpu.HBM)
    f32, bf16 = jnp.float32, jnp.bfloat16
    rows = comps * fab_local
    flat_b, flat_t = pl.pallas_call(
        functools.partial(kernel, plan_b, plan_t, table_b, table_t),
        out_shape=[
            jax.ShapeDtypeStruct((plan_b.total, LANES), f32),
            jax.ShapeDtypeStruct((plan_t.total, LANES), f32),
        ],
        in_specs=[hbm] * 9,
        out_specs=[hbm] * 2,
        scratch_shapes=[
            *[
                pltpu.VMEM(x.shape, f32)
                for x in (fabric_params, query_points, cot, b1, b2, b3, t1, t2, t3)
            ],
            pltpu.SemaphoreType.DMA((9,)),
            pltpu.SemaphoreType.DMA((2,)),
            pltpu.VMEM((rows, points), bf16),
            pltpu.VMEM((rows, points), bf16),
            pltpu.VMEM((width, rows), bf16),
            pltpu.VMEM((width, rows), bf16),
            pltpu.VMEM((hidden, points), bf16),
            pltpu.VMEM((hidden, points), bf16),
            pltpu.VMEM((hidden, points), bf16),
            pltpu.VMEM((hidden, points), bf16),
            pltpu.VMEM((hidden, points), f32),
            pltpu.VMEM((hidden, points), f32),
            pltpu.VMEM((width, points), f32),
            pltpu.VMEM((2,) + t2.shape, bf16),
            pltpu.VMEM((2,) + t3.shape, bf16),
            pltpu.VMEM((2,) + t2.shape[::-1], bf16),
            pltpu.VMEM((2,) + t3.shape[::-1], bf16),
            pltpu.VMEM((hidden, 8), f32),
            pltpu.VMEM((8, points), f32),
            pltpu.VMEM((rows, width), f32),
            pltpu.VMEM((8, hidden), f32),
            pltpu.VMEM(t2.shape, f32),
            pltpu.VMEM(t3.shape, f32),
        ]
        + plan_b.scratch()
        + plan_t.scratch(),
        compiler_params=pltpu.CompilerParams(
            collective_id=0, has_side_effects=True, vmem_limit_bytes=50 * 1024 * 1024
        ),
    )(fabric_params, query_points, cot, b1, b2, b3, t1, t2, t3)
    return tuple(
        pl.pallas_call(
            functools.partial(unpack, (table_b, table_t), (group_b, group_t)),
            out_shape=[jax.ShapeDtypeStruct(s, f32) for s in shapes],
            in_specs=[hbm] * 2,
            out_specs=[vmem] * 6,
            scratch_shapes=[
                pltpu.VMEM((plan_b.total, LANES), f32),
                pltpu.VMEM((plan_t.total, LANES), f32),
                pltpu.SemaphoreType.DMA((2,)),
            ],
        )(flat_b, flat_t)
    )


def solution(mesh):
    nf = mesh.shape["fab"]
    nq = mesh.shape["pts"] // 2
    return jax.shard_map(
        functools.partial(local, nf, nq),
        mesh=mesh,
        in_specs=(
            P(None, "fab"),
            P(None, "pts"),
            P(None, "fab", "pts"),
            P(),
            P(),
            P(),
            P(),
            P(),
            P(),
        ),
        out_specs=(P(), P(), P(), P(), P(), P()),
        check_vma=False,
    )
```
